32 devices in a mesh: group: 4 (over y, x), local: 8 (over z, core).
Axes of the slice: x: 2, y: 2, z: 4, core: 2. Of those that a mesh axis runs over, the one named last changes fastest.
Arguments:
- features: bfloat16 [192, 7168], P(('group', 'local')), may hold values from -6 to 6
- cotangent: bfloat16 [192, 7168], P(('group', 'local')), may hold values from -6 to 6
- expert_ids: int32 [192, 4], P(('group', 'local')), may hold values from 0 to 7, as said below
- gates: float32 [192, 4], P(('group', 'local')), may hold values from 0.1 to 1
- w_gate: bfloat16 [8, 7168, 2048], P('local', None, 'group'), may hold values from -0.0625 to 0.0625
- w_up: bfloat16 [8, 7168, 2048], P('local', None, 'group'), may hold values from -0.0625 to 0.0625
- w_down: bfloat16 [8, 2048, 7168], P('local', 'group'), may hold values from -0.125 to 0.125
Outputs:
- grad_features: float32 [192, 7168], P(('group', 'local'))
- grad_gate: bfloat16 [8, 7168, 2048], P('local', None, 'group')
- grad_up: bfloat16 [8, 7168, 2048], P('local', None, 'group')
- grad_down: bfloat16 [8, 2048, 7168], P('local', 'group')
The draws below stay inside these ranges and needn't reach their ends.
Inputs may be any that keep to these rules, and one draw needn't show every extreme that they name: `expert_ids`: each row names 4 different experts, all of them in at most 3 expert groups, expert e lying in group e // 2.
All inputs are finite; a program needn't handle non-finite values.
Results may differ from the reference program's by a relative error of at most 0.013.
Values may be sent and summed in bfloat16 or wider, within the bound.
A program may use at most 192 MiB of HBM per device.

```python
import math
import jax
import jax.numpy as jnp
from jax import lax

D = 7168
FF = 2048
EPG = 2
TOPG = 3
TOPK = 4
TOK_DEV = 6
EXPERTS = 8
NBLK = 32
TOKENS = 192
CAP = 6
N_GROUP = 4


def draw_expert_ids(key, part):
    key_groups = jax.random.fold_in(key, 11)
    key_experts = jax.random.fold_in(key, 12)
    key_bias = jax.random.fold_in(key, 13)
    key_gbias = jax.random.fold_in(key, 14)
    group_count = EXPERTS // EPG
    group_bias = jax.random.randint(key_gbias, (group_count,), 0, 3) * 16384
    group_score = (jax.random.randint(key_groups, (TOKENS, group_count), 0, 32768) + group_bias[None, :]) * group_count
    group_score = group_score + jnp.arange(group_count, dtype=jnp.int32)[None, :]
    unused, chosen = lax.top_k(group_score, TOPG)
    expert_group = jnp.arange(EXPERTS, dtype=jnp.int32) // EPG
    allowed = jnp.any(expert_group[None, None, :] == chosen[:, :, None], axis=1)
    expert_bias = jax.random.randint(key_bias, (EXPERTS,), 0, 3) * 16384
    expert_score = (jax.random.randint(key_experts, (TOKENS, EXPERTS), 0, 32768) + expert_bias[None, :]) * EXPERTS
    expert_score = expert_score + jnp.arange(EXPERTS, dtype=jnp.int32)[None, :]
    expert_score = jnp.where(allowed, expert_score, -1)
    unused_two, picked = lax.top_k(expert_score, TOPK)
    return picked.astype(jnp.int32)


def level_of(rng, shape, split, smallest, largest):
    def one(axis_at, parts):
        draws = jax.random.uniform(jax.random.fold_in(jax.random.fold_in(rng, 6), axis_at), (parts,), jnp.float32, smallest / len(split), largest / len(split))
        return jnp.repeat(jnp.exp(draws), shape[axis_at] // parts).reshape((-1,) + (1,) * (len(shape) - axis_at - 1))

    gain = one(*split[0])
    for cut in split[1:]:
        gain = gain * one(*cut)
    return gain


def scatter_about(stream_key, shape, scale, limit, split=(), held_as=jnp.bfloat16):
    entries = jax.random.normal(stream_key, shape, jnp.float32) * scale
    if len(split) > 0:
        entries = level_of(stream_key, shape, split, -0.22, 0.18) * entries
    return jnp.clip(entries, min=-limit, max=limit).astype(held_as)


def setup_inputs(seed: int = 0) -> dict:
    key_of = jax.random.split(jax.random.key(seed), 8)
    return {
        "features": scatter_about(key_of[0], (TOKENS, D), 1.0, 6.0, ((0, 32),)),
        "cotangent": scatter_about(key_of[1], (TOKENS, D), 1.0, 6.0, ((0, 32),)),
        "expert_ids": draw_expert_ids(jax.random.fold_in(key_of[7], 71), 0),
        "gates": jnp.clip(jnp.exp(math.log(1.0) - 2.3025851 * jax.random.uniform(key_of[3], (TOKENS, TOPK), jnp.float32) ** level_of(key_of[3], (TOKENS, TOPK), ((0, 32),), -0.2, 0.2)), 0.1, 1.0),
        "w_gate": scatter_about(key_of[4], (EXPERTS, D, FF), D ** -0.5, 0.0625, ((0, 8), (2, 4))),
        "w_up": scatter_about(key_of[5], (EXPERTS, D, FF), D ** -0.5, 0.0625, ((0, 8), (2, 4))),
        "w_down": scatter_about(key_of[6], (EXPERTS, FF, D), FF ** -0.5, 0.125, ((0, 8), (1, 4))),
    }


def silu_parts(pre):
    sig = jax.nn.sigmoid(pre)
    return pre * sig, sig * (1.0 + pre * (1.0 - sig))


def slot_table(expert_ids):
    blocks = expert_ids.reshape(NBLK, TOK_DEV, TOPK)
    hits = (blocks[..., None] == jnp.arange(EXPERTS, dtype=jnp.int32)).astype(jnp.int32)
    counts = jnp.sum(hits, axis=2)
    before = jnp.cumsum(counts, axis=1) - counts
    slots = jnp.sum(hits * before[:, :, None, :], axis=3)
    return slots.reshape(TOKENS, TOPK).astype(jnp.int32)


def reference(features, cotangent, expert_ids, gates, w_gate, w_up, w_down):
    slots = slot_table(expert_ids)
    kept = slots < CAP
    token = jnp.arange(TOKENS, dtype=jnp.int32)
    block = token // TOK_DEV
    total = EXPERTS * NBLK * CAP
    where = (expert_ids * NBLK + block[:, None]) * CAP + jnp.minimum(slots, CAP - 1)
    where = jnp.where(kept, where, total).astype(jnp.int32)
    flat_where = where.reshape(-1)
    owners = jnp.broadcast_to(token[:, None], (TOKENS, TOPK)).reshape(-1)
    source = jnp.full((total + 1,), TOKENS, jnp.int32).at[flat_where].set(owners)
    weight = jnp.zeros((total + 1,), jnp.float32).at[flat_where].set(gates.reshape(-1))
    source = source[:total].reshape(EXPERTS, NBLK * CAP)
    weight = weight[:total].reshape(EXPERTS, NBLK * CAP)
    padded_x = jnp.concatenate([features, jnp.zeros((1, D), features.dtype)], axis=0)
    padded_g = jnp.concatenate([cotangent, jnp.zeros((1, D), cotangent.dtype)], axis=0)
    slice_width = FF // N_GROUP

    def expert(index):
        rows = source[index]
        bin_x = padded_x[rows]
        bin_g = (weight[index][:, None] * padded_g[rows].astype(jnp.float32)).astype(jnp.bfloat16)
        gate_w = w_gate[index]
        up_w = w_up[index]
        down_w = w_down[index]
        pre_gate = jnp.dot(bin_x, gate_w, preferred_element_type=jnp.float32)
        pre_up = jnp.dot(bin_x, up_w, preferred_element_type=jnp.float32)
        act, slope = silu_parts(pre_gate)
        hidden = (act * pre_up).astype(jnp.bfloat16)
        grad_down = jnp.dot(hidden.T, bin_g, preferred_element_type=jnp.float32).astype(jnp.bfloat16)
        d_hidden = jnp.dot(bin_g, down_w.T, preferred_element_type=jnp.float32)
        d_gate = (d_hidden * pre_up * slope).astype(jnp.bfloat16)
        d_up = (d_hidden * act).astype(jnp.bfloat16)
        grad_gate = jnp.dot(bin_x.T, d_gate, preferred_element_type=jnp.float32).astype(jnp.bfloat16)
        grad_up = jnp.dot(bin_x.T, d_up, preferred_element_type=jnp.float32).astype(jnp.bfloat16)
        summed = jnp.zeros((NBLK * CAP, D), jnp.float32)
        for piece_index in range(N_GROUP):
            low = piece_index * slice_width
            high = low + slice_width
            piece = jnp.dot(d_gate[:, low:high], gate_w[:, low:high].T, preferred_element_type=jnp.float32)
            piece = piece + jnp.dot(d_up[:, low:high], up_w[:, low:high].T, preferred_element_type=jnp.float32)
            rounded = lax.optimization_barrier(piece.astype(jnp.bfloat16))
            summed = summed + rounded.astype(jnp.float32)
        return grad_gate, grad_up, grad_down, summed

    grad_gate, grad_up, grad_down, bin_dx = lax.map(expert, jnp.arange(EXPERTS, dtype=jnp.int32))
    flat_dx = jnp.concatenate([bin_dx.reshape(total, D), jnp.zeros((1, D), jnp.float32)], axis=0)
    grad_features = jnp.sum(flat_dx[where], axis=1)
    return grad_features, grad_gate, grad_up, grad_down
```

```python
import jax
import jax.numpy as jnp
from jax import lax
from jax.sharding import PartitionSpec as P

BOTH = ("group", "local")


def silu_parts(pre):
    sig = jax.nn.sigmoid(pre)
    return (pre * sig, sig * (1.0 + pre * (1.0 - sig)))


def body(features, cotangent, expert_ids, gates, w_gate, w_up, w_down):
    experts = lax.axis_size("local")
    devices = experts * lax.axis_size("group")
    tok_rows, width = features.shape
    rows = devices * tok_rows
    hits = expert_ids[..., None] == jnp.arange(experts, dtype=jnp.int32)
    on = jnp.sum(hits.astype(jnp.float32), axis=1)
    weight = jnp.sum(jnp.where(hits, gates[..., None], 0.0), axis=1)
    routes = lax.all_gather(jnp.concatenate([on, weight], axis=1)[None], BOTH, axis=0, tiled=True)
    all_x = lax.all_gather(features[None], BOTH, axis=0, tiled=True)
    all_g = lax.all_gather(cotangent[None], BOTH, axis=0, tiled=True)
    me = lax.axis_index("local")
    routes = routes.reshape(rows, 2 * experts)
    on = lax.dynamic_slice_in_dim(routes, me, 1, axis=1)
    weight = lax.dynamic_slice_in_dim(routes, me + experts, 1, axis=1)
    rows_x = jnp.where(on > 0.0, all_x.reshape(rows, width), jnp.bfloat16(0))
    rows_g = (weight * all_g.reshape(rows, width).astype(jnp.float32)).astype(jnp.bfloat16)
    gate_w = w_gate[0]
    up_w = w_up[0]
    down_w = w_down[0]
    pre_gate = jnp.dot(rows_x, gate_w, preferred_element_type=jnp.float32)
    pre_up = jnp.dot(rows_x, up_w, preferred_element_type=jnp.float32)
    act, slope = silu_parts(pre_gate)
    hidden = (act * pre_up).astype(jnp.bfloat16)
    d_hidden = jnp.dot(rows_g, down_w.T, preferred_element_type=jnp.float32)
    d_gate = (d_hidden * pre_up * slope).astype(jnp.bfloat16)
    d_up = (d_hidden * act).astype(jnp.bfloat16)
    part = jnp.dot(d_gate, gate_w.T, preferred_element_type=jnp.float32)
    part = part + jnp.dot(d_up, up_w.T, preferred_element_type=jnp.float32)
    part = lax.optimization_barrier(part.astype(jnp.bfloat16))
    summed = lax.psum_scatter(
        part.reshape(devices, tok_rows, width), BOTH, scatter_dimension=0, tiled=True
    )
    grad_down = jnp.dot(hidden.T, rows_g, preferred_element_type=jnp.float32).astype(jnp.bfloat16)
    grad_gate = jnp.dot(rows_x.T, d_gate, preferred_element_type=jnp.float32).astype(jnp.bfloat16)
    grad_up = jnp.dot(rows_x.T, d_up, preferred_element_type=jnp.float32).astype(jnp.bfloat16)
    return (summed[0].astype(jnp.float32), grad_gate[None], grad_up[None], grad_down[None])


def solution(mesh):
    tokens = P(BOTH, None)
    wide = P("local", None, "group")
    tall = P("local", "group", None)
    return jax.shard_map(
        body,
        mesh=mesh,
        in_specs=(tokens, tokens, tokens, tokens, wide, wide, tall),
        out_specs=(tokens, wide, wide, tall),
        check_vma=False,
    )
```

```python
import functools

import jax
import jax.numpy as jnp
from jax import lax
from jax.experimental import pallas as pl
from jax.experimental.pallas import tpu as pltpu
from jax.sharding import PartitionSpec as P

BOTH = ("group", "local")
MESH = pl.DeviceIdType.MESH
ROWS = 8
EXTRA = 128


def place(groups, local):
    me_g, me_l = lax.axis_index("group"), lax.axis_index("local")
    z, core = me_l // 2, me_l % 2
    zs = local // 2
    g_at = lambda d: lax.rem(me_g + d, groups)
    z_at = lambda d: lax.rem(z + d, zs)
    sibling = (me_g, z * 2 + 1 - core)
    by_group = lambda d: (g_at(d), me_l)
    by_z = lambda d: (me_g, z_at(d) * 2 + core)
    return core, zs, g_at, z_at, sibling, by_group, by_z


def greet(groups, zs, sibling, by_group, by_z):
    peers = [sibling]
    peers += [by_group(d) for d in range(1, groups)]
    peers += [by_z(d) for d in range(1, zs)]
    barrier = pltpu.get_barrier_semaphore()
    for peer in peers:
        pl.semaphore_signal(barrier, inc=1, device_id=peer, device_id_type=MESH)
    pl.semaphore_wait(barrier, len(peers))


def gather_kernel(groups, local, x_in, g_in, x_out, g_out, own_sem, send_sem, recv_sem):
    core, zs, g_at, z_at, sibling, by_group, by_z = place(groups, local)
    pairs = ((x_in, x_out), (g_in, g_out))
    slot = lambda d, e, c: g_at(d) * local + z_at(e) * 2 + c
    greet(groups, zs, sibling, by_group, by_z)
    mine = slot(0, 0, core)
    sent = []

    def send(a, src, at, msg, peer):
        copy = pltpu.make_async_remote_copy(
            src_ref=src, dst_ref=pairs[a][1].at[at], send_sem=send_sem.at[a, msg],
            recv_sem=recv_sem.at[a, at], device_id=peer, device_id_type=MESH,
        )
        copy.start()
        sent.append(copy)

    def arrived(a, at):
        block = pairs[a][1].at[at]
        pltpu.make_async_remote_copy(
            src_ref=block, dst_ref=block, send_sem=send_sem.at[a, 0],
            recv_sem=recv_sem.at[a, at], device_id=sibling, device_id_type=MESH,
        ).wait_recv()

    first_group = zs - 1
    first_core = first_group + zs * (groups - 1)
    keeps = []
    for a in range(2):
        keep = pltpu.make_async_copy(pairs[a][0], pairs[a][1].at[mine], own_sem.at[a])
        keep.start()
        keeps.append(keep)
        for e in range(1, zs):
            send(a, pairs[a][0], mine, e - 1, by_z(e))
        for d in range(1, groups):
            send(a, pairs[a][0], mine, first_group + d - 1, by_group(d))
        send(a, pairs[a][0], mine, first_core, sibling)
    for a in range(2):
        for e in range(1, zs):
            at = slot(0, e, core)
            arrived(a, at)
            for d in range(1, groups):
                send(a, pairs[a][1].at[at], at, first_group + e * (groups - 1) + d - 1, by_group(d))
            send(a, pairs[a][1].at[at], at, first_core + e, sibling)
    for a in range(2):
        for e in range(zs):
            for d in range(1, groups):
                at = slot(d, e, core)
                arrived(a, at)
                send(a, pairs[a][1].at[at], at, first_core + d * zs + e, sibling)
    for a in range(2):
        for d in range(groups):
            for e in range(zs):
                arrived(a, slot(d, e, 1 - core))
    for copy in sent:
        copy.wait_send()
    for keep in keeps:
        keep.wait()


def reduce_kernel(
    groups, local, part, out, recv_core, sum_core, recv_group, sum_z, recv_z,
    send1, got1, send2, got2, send3, got3,
):
    core, zs, g_at, z_at, sibling, by_group, by_z = place(groups, local)
    slot = lambda d, e, c: g_at(d) * local + z_at(e) * 2 + c
    greet(groups, zs, sibling, by_group, by_z)
    f32 = jnp.float32
    order = [(d, e) for e in list(range(1, zs)) + [0] for d in list(range(1, groups)) + [0]]

    def send(src, dst, s_sem, r_sem, peer):
        copy = pltpu.make_async_remote_copy(
            src_ref=src, dst_ref=dst, send_sem=s_sem, recv_sem=r_sem,
            device_id=peer, device_id_type=MESH,
        )
        copy.start()
        return copy

    first = {}
    for d, e in order:
        k = d * zs + e
        first[k] = send(
            part.at[slot(d, e, 1 - core)], recv_core.at[k], send1.at[k], got1.at[k], sibling
        )
    second = {}
    for d, e in order:
        if d == 0:
            continue
        k = d * zs + e
        first[k].wait_recv()
        both = part[slot(d, e, core)].astype(f32) + recv_core[k].astype(f32)
        sum_core[k - zs] = both.astype(sum_core.dtype)
        second[k] = send(
            sum_core.at[k - zs], recv_group.at[k - zs], send2.at[k - zs], got2.at[k - zs], by_group(d)
        )
    third = []
    for e in list(range(1, zs)) + [0]:
        first[e].wait_recv()
        total = part[slot(0, e, core)].astype(f32) + recv_core[e].astype(f32)
        for d in range(1, groups):
            k = d * zs + e
            second[k].wait_recv()
            total = total + recv_group[k - zs].astype(f32)
        if e == 0:
            out[...] = total
        else:
            sum_z[e - 1] = total.astype(sum_z.dtype)
            third.append(
                send(sum_z.at[e - 1], recv_z.at[e - 1], send3.at[e - 1], got3.at[e - 1], by_z(e))
            )
    for e in range(1, zs):
        third[e - 1].wait_recv()
        out[...] += recv_z[e - 1].astype(f32)
    for copy in [*first.values(), *second.values(), *third]:
        copy.wait_send()


def gather(groups, local, x, g):
    n = groups * local
    zs = local // 2
    messages = zs - 1 + zs * (groups - 1) + zs * groups
    anywhere = pl.BlockSpec(memory_space=pl.ANY)
    return pl.pallas_call(
        functools.partial(gather_kernel, groups, local),
        out_shape=(
            jax.ShapeDtypeStruct((n,) + x.shape, x.dtype),
            jax.ShapeDtypeStruct((n,) + g.shape, g.dtype),
        ),
        in_specs=[anywhere] * 2,
        out_specs=(anywhere, anywhere),
        scratch_shapes=[
            pltpu.SemaphoreType.DMA((2,)),
            pltpu.SemaphoreType.DMA((2, messages)),
            pltpu.SemaphoreType.DMA((2, n)),
        ],
        compiler_params=pltpu.CompilerParams(collective_id=0, has_side_effects=True),
        name="gather",
    )(x, g)


def reduce(groups, local, part):
    zs = local // 2
    block = part.shape[1:]
    slots = lambda k: pltpu.VMEM((k,) + block, part.dtype)
    near, far = zs * groups, zs * (groups - 1)
    dma = pltpu.SemaphoreType.DMA
    return pl.pallas_call(
        functools.partial(reduce_kernel, groups, local),
        out_shape=jax.ShapeDtypeStruct(block, jnp.float32),
        in_specs=[pl.BlockSpec(memory_space=pltpu.VMEM)],
        out_specs=pl.BlockSpec(memory_space=pltpu.VMEM),
        scratch_shapes=[
            slots(near), slots(far), slots(far), slots(zs - 1), slots(zs - 1),
            dma((near,)), dma((near,)), dma((far,)), dma((far,)), dma((zs - 1,)), dma((zs - 1,)),
        ],
        compiler_params=pltpu.CompilerParams(
            collective_id=1, has_side_effects=True, vmem_limit_bytes=50 * 2**20
        ),
        name="reduce",
    )(part)


def silu_parts(pre):
    sig = jax.nn.sigmoid(pre)
    return (pre * sig, sig * (1.0 + pre * (1.0 - sig)))


def body(features, cotangent, expert_ids, gates, w_gate, w_up, w_down):
    local = lax.axis_size("local")
    groups = lax.axis_size("group")
    tok_rows, width = features.shape
    rows = groups * local * ROWS
    pad = ROWS - tok_rows
    hits = expert_ids[..., None] == jnp.arange(local, dtype=jnp.int32)
    weight = jnp.sum(jnp.where(hits, gates[..., None], 0.0), axis=1)
    high = lax.reduce_precision(weight, 8, 7)
    middle = lax.reduce_precision(weight - high, 8, 7)
    low = weight - high - middle
    terms = jnp.concatenate([high, middle, low], axis=1).astype(jnp.bfloat16)
    terms = jnp.pad(terms, ((0, 0), (0, EXTRA - 3 * local)))
    x = jnp.pad(features, ((0, pad), (0, 0)))
    g = jnp.pad(jnp.concatenate([cotangent, terms], axis=1), ((0, pad), (0, 0)))
    all_x, all_g = gather(groups, local, x, g)
    rows_x = all_x.reshape(rows, width)
    all_g = all_g.reshape(rows, width + EXTRA)
    terms = all_g[:, width : width + 3 * local].astype(jnp.float32).reshape(rows, 3, local)
    mine = jnp.arange(local) == lax.axis_index("local")
    terms = jnp.sum(jnp.where(mine, terms, 0.0), axis=2)
    weight = (terms[:, 0] + terms[:, 1] + terms[:, 2])[:, None]
    rows_g = (weight * all_g[:, :width].astype(jnp.float32)).astype(jnp.bfloat16)
    gate_w = w_gate[0]
    up_w = w_up[0]
    down_w = w_down[0]
    pre_gate = jnp.dot(rows_x, gate_w, preferred_element_type=jnp.float32)
    pre_up = jnp.dot(rows_x, up_w, preferred_element_type=jnp.float32)
    act, slope = silu_parts(pre_gate)
    hidden = (act * pre_up).astype(jnp.bfloat16)
    d_hidden = jnp.dot(rows_g, down_w.T, preferred_element_type=jnp.float32)
    d_gate = (d_hidden * pre_up * slope).astype(jnp.bfloat16)
    d_up = (d_hidden * act).astype(jnp.bfloat16)
    part = jnp.dot(d_gate, gate_w.T, preferred_element_type=jnp.float32)
    part = part + jnp.dot(d_up, up_w.T, preferred_element_type=jnp.float32)
    part = part.astype(jnp.bfloat16).reshape(groups * local, ROWS, width)
    summed = reduce(groups, local, part)
    grad_down = jnp.dot(hidden.T, rows_g, preferred_element_type=jnp.float32).astype(jnp.bfloat16)
    grad_gate = jnp.dot(rows_x.T, d_gate, preferred_element_type=jnp.float32).astype(jnp.bfloat16)
    grad_up = jnp.dot(rows_x.T, d_up, preferred_element_type=jnp.float32).astype(jnp.bfloat16)
    return (summed[:tok_rows], grad_gate[None], grad_up[None], grad_down[None])


def solution(mesh):
    tokens = P(BOTH, None)
    wide = P("local", None, "group")
    tall = P("local", "group", None)
    return jax.shard_map(
        body,
        mesh=mesh,
        in_specs=(tokens, tokens, tokens, tokens, wide, wide, tall),
        out_specs=(tokens, wide, wide, tall),
        check_vma=False,
    )
```

```python
import functools

import jax
import jax.numpy as jnp
from jax import lax
from jax.experimental import pallas as pl
from jax.experimental.pallas import tpu as pltpu
from jax.sharding import PartitionSpec as P

BOTH = ("group", "local")
MESH = pl.DeviceIdType.MESH
ROWS = 8
EXTRA = 128


def place(groups, local):
    me_g, me_l = lax.axis_index("group"), lax.axis_index("local")
    z, core = me_l // 2, me_l % 2
    zs = local // 2
    g_at = lambda d: lax.rem(me_g + d, groups)
    if groups == 4:
        across, along = me_g // 2, me_g % 2
        g_at = lambda d: (
            me_g, across * 2 + 1 - along, (1 - across) * 2 + along, (1 - across) * 2 + 1 - along
        )[d]
    z_at = lambda d: lax.rem(z + d, zs)
    sibling = (me_g, z * 2 + 1 - core)
    by_group = lambda d: (g_at(d), me_l)
    by_z = lambda d: (me_g, z_at(d) * 2 + core)
    return core, zs, g_at, z_at, sibling, by_group, by_z


def greet(groups, zs, sibling, by_group, by_z):
    peers = [sibling]
    peers += [by_group(d) for d in range(1, groups)]
    peers += [by_z(d) for d in range(1, zs)]
    barrier = pltpu.get_barrier_semaphore()
    for peer in peers:
        pl.semaphore_signal(barrier, inc=1, device_id=peer, device_id_type=MESH)
    pl.semaphore_wait(barrier, len(peers))


def gather_kernel(groups, local, x_in, g_in, x_out, g_out, own_sem, send_sem, recv_sem):
    core, zs, g_at, z_at, sibling, by_group, by_z = place(groups, local)
    pairs = ((x_in, x_out), (g_in, g_out))
    slot = lambda d, e, c: g_at(d) * local + z_at(e) * 2 + c
    greet(groups, zs, sibling, by_group, by_z)
    mine = slot(0, 0, core)
    sent = []

    def send(a, src, at, msg, peer):
        copy = pltpu.make_async_remote_copy(
            src_ref=src, dst_ref=pairs[a][1].at[at], send_sem=send_sem.at[a, msg],
            recv_sem=recv_sem.at[a, at], device_id=peer, device_id_type=MESH,
        )
        copy.start()
        sent.append(copy)

    def arrived(a, at):
        block = pairs[a][1].at[at]
        pltpu.make_async_remote_copy(
            src_ref=block, dst_ref=block, send_sem=send_sem.at[a, 0],
            recv_sem=recv_sem.at[a, at], device_id=sibling, device_id_type=MESH,
        ).wait_recv()

    first_group = zs - 1
    first_core = first_group + zs * (groups - 1)
    keeps = []
    relayed = groups == 4
    direct = range(1, 3 if relayed else groups)

    def relay(a, at, d, e):
        if relayed and d == 1 + e % 2:
            send(a, pairs[a][1].at[at], at, first_group + e * (groups - 1) + 2, by_group(3 - d))

    def pass_on(a, d, e):
        at = slot(d, e, core)
        arrived(a, at)
        relay(a, at, d, e)
        send(a, pairs[a][1].at[at], at, first_core + d * zs + e, sibling)

    for a in range(2):
        keep = pltpu.make_async_copy(pairs[a][0], pairs[a][1].at[mine], own_sem.at[a])
        keep.start()
        keeps.append(keep)
        for e in range(1, zs):
            send(a, pairs[a][0], mine, e - 1, by_z(e))
        for d in direct:
            send(a, pairs[a][0], mine, first_group + d - 1, by_group(d))
        send(a, pairs[a][0], mine, first_core, sibling)
    for a in range(2):
        for e in range(1, zs):
            at = slot(0, e, core)
            arrived(a, at)
            for d in direct:
                send(a, pairs[a][1].at[at], at, first_group + e * (groups - 1) + d - 1, by_group(d))
            send(a, pairs[a][1].at[at], at, first_core + e, sibling)
        for d in direct:
            pass_on(a, d, 0)
    for a in range(2):
        for e in range(1, zs):
            for d in direct:
                pass_on(a, d, e)
    for a in range(2):
        for e in range(zs):
            for d in range(3 if relayed else groups, groups):
                pass_on(a, d, e)
    for a in range(2):
        for d in range(groups):
            for e in range(zs):
                arrived(a, slot(d, e, 1 - core))
    for copy in sent:
        copy.wait_send()
    for keep in keeps:
        keep.wait()


def reduce_kernel(
    groups, local, part, out, recv_core, sum_core, recv_group, sum_z, recv_z,
    send1, got1, send2, got2, send3, got3,
):
    core, zs, g_at, z_at, sibling, by_group, by_z = place(groups, local)
    slot = lambda d, e, c: g_at(d) * local + z_at(e) * 2 + c
    greet(groups, zs, sibling, by_group, by_z)
    f32 = jnp.float32
    order = [(d, e) for e in list(range(1, zs)) + [0] for d in list(range(groups - 1, 0, -1)) + [0]]

    def send(src, dst, s_sem, r_sem, peer):
        copy = pltpu.make_async_remote_copy(
            src_ref=src, dst_ref=dst, send_sem=s_sem, recv_sem=r_sem,
            device_id=peer, device_id_type=MESH,
        )
        copy.start()
        return copy

    first = {}
    for d, e in order:
        k = d * zs + e
        first[k] = send(
            part.at[slot(d, e, 1 - core)], recv_core.at[k], send1.at[k], got1.at[k], sibling
        )
    second = {}
    relayed = groups == 4

    def add_and_send(d, e, extra, peer):
        k = d * zs + e
        first[k].wait_recv()
        both = part[slot(d, e, core)].astype(f32) + recv_core[k].astype(f32)
        if extra:
            second[3 * zs + e].wait_recv()
            both = both + recv_group[2 * zs + e].astype(f32)
        sum_core[k - zs] = both.astype(sum_core.dtype)
        second[k] = send(
            sum_core.at[k - zs], recv_group.at[k - zs], send2.at[k - zs], got2.at[k - zs], by_group(peer)
        )

    late = list(range(1, zs)) + [0]
    if relayed:
        for e in late:
            add_and_send(3, e, False, 1 + e % 2)
            add_and_send(1 + e % 2, e, False, 1 + e % 2)
        for e in late:
            add_and_send(2 - e % 2, e, True, 2 - e % 2)
    else:
        for d, e in order:
            if d:
                add_and_send(d, e, False, d)
    third = []
    for e in list(range(1, zs)) + [0]:
        first[e].wait_recv()
        total = part[slot(0, e, core)].astype(f32) + recv_core[e].astype(f32)
        for d in range(1, 3 if relayed else groups):
            k = d * zs + e
            second[k].wait_recv()
            total = total + recv_group[k - zs].astype(f32)
        if e == 0:
            out[...] = total
        else:
            sum_z[e - 1] = total.astype(sum_z.dtype)
            third.append(
                send(sum_z.at[e - 1], recv_z.at[e - 1], send3.at[e - 1], got3.at[e - 1], by_z(e))
            )
    for e in range(1, zs):
        third[e - 1].wait_recv()
        out[...] += recv_z[e - 1].astype(f32)
    for copy in [*first.values(), *second.values(), *third]:
        copy.wait_send()


def gather(groups, local, x, g):
    n = groups * local
    zs = local // 2
    messages = zs - 1 + zs * (groups - 1) + zs * groups
    anywhere = pl.BlockSpec(memory_space=pl.ANY)
    return pl.pallas_call(
        functools.partial(gather_kernel, groups, local),
        out_shape=(
            jax.ShapeDtypeStruct((n,) + x.shape, x.dtype),
            jax.ShapeDtypeStruct((n,) + g.shape, g.dtype),
        ),
        in_specs=[anywhere] * 2,
        out_specs=(anywhere, anywhere),
        scratch_shapes=[
            pltpu.SemaphoreType.DMA((2,)),
            pltpu.SemaphoreType.DMA((2, messages)),
            pltpu.SemaphoreType.DMA((2, n)),
        ],
        compiler_params=pltpu.CompilerParams(collective_id=0, has_side_effects=True),
        name="gather",
    )(x, g)


def reduce(groups, local, part):
    zs = local // 2
    block = part.shape[1:]
    slots = lambda k: pltpu.VMEM((k,) + block, part.dtype)
    near, far = zs * groups, zs * (groups - 1)
    dma = pltpu.SemaphoreType.DMA
    return pl.pallas_call(
        functools.partial(reduce_kernel, groups, local),
        out_shape=jax.ShapeDtypeStruct(block, jnp.float32),
        in_specs=[pl.BlockSpec(memory_space=pltpu.VMEM)],
        out_specs=pl.BlockSpec(memory_space=pltpu.VMEM),
        scratch_shapes=[
            slots(near), slots(far), slots(far), slots(zs - 1), slots(zs - 1),
            dma((near,)), dma((near,)), dma((far,)), dma((far,)), dma((zs - 1,)), dma((zs - 1,)),
        ],
        compiler_params=pltpu.CompilerParams(
            collective_id=1, has_side_effects=True, vmem_limit_bytes=50 * 2**20
        ),
        name="reduce",
    )(part)


def silu_parts(pre):
    sig = jax.nn.sigmoid(pre)
    return (pre * sig, sig * (1.0 + pre * (1.0 - sig)))


def body(features, cotangent, expert_ids, gates, w_gate, w_up, w_down):
    local = lax.axis_size("local")
    groups = lax.axis_size("group")
    tok_rows, width = features.shape
    rows = groups * local * ROWS
    pad = ROWS - tok_rows
    hits = expert_ids[..., None] == jnp.arange(local, dtype=jnp.int32)
    weight = jnp.sum(jnp.where(hits, gates[..., None], 0.0), axis=1)
    high = lax.reduce_precision(weight, 8, 7)
    middle = lax.reduce_precision(weight - high, 8, 7)
    low = weight - high - middle
    terms = jnp.concatenate([high, middle, low], axis=1).astype(jnp.bfloat16)
    terms = jnp.pad(terms, ((0, 0), (0, EXTRA - 3 * local)))
    x = jnp.pad(features, ((0, pad), (0, 0)))
    g = jnp.pad(jnp.concatenate([cotangent, terms], axis=1), ((0, pad), (0, 0)))
    all_x, all_g = gather(groups, local, x, g)
    rows_x = all_x.reshape(rows, width)
    all_g = all_g.reshape(rows, width + EXTRA)
    terms = all_g[:, width : width + 3 * local].astype(jnp.float32).reshape(rows, 3, local)
    mine = jnp.arange(local) == lax.axis_index("local")
    terms = jnp.sum(jnp.where(mine, terms, 0.0), axis=2)
    weight = (terms[:, 0] + terms[:, 1] + terms[:, 2])[:, None]
    rows_g = (weight * all_g[:, :width].astype(jnp.float32)).astype(jnp.bfloat16)
    gate_w = w_gate[0]
    up_w = w_up[0]
    down_w = w_down[0]
    pre_gate = jnp.dot(rows_x, gate_w, preferred_element_type=jnp.float32)
    pre_up = jnp.dot(rows_x, up_w, preferred_element_type=jnp.float32)
    act, slope = silu_parts(pre_gate)
    hidden = (act * pre_up).astype(jnp.bfloat16)
    d_hidden = jnp.dot(rows_g, down_w.T, preferred_element_type=jnp.float32)
    d_gate = (d_hidden * pre_up * slope).astype(jnp.bfloat16)
    d_up = (d_hidden * act).astype(jnp.bfloat16)
    part = jnp.dot(d_gate, gate_w.T, preferred_element_type=jnp.float32)
    part = part + jnp.dot(d_up, up_w.T, preferred_element_type=jnp.float32)
    part = part.astype(jnp.bfloat16).reshape(groups * local, ROWS, width)
    summed = reduce(groups, local, part)
    grad_down = jnp.dot(hidden.T, rows_g, preferred_element_type=jnp.float32).astype(jnp.bfloat16)
    grad_gate = jnp.dot(rows_x.T, d_gate, preferred_element_type=jnp.float32).astype(jnp.bfloat16)
    grad_up = jnp.dot(rows_x.T, d_up, preferred_element_type=jnp.float32).astype(jnp.bfloat16)
    return (summed[:tok_rows], grad_gate[None], grad_up[None], grad_down[None])


def solution(mesh):
    tokens = P(BOTH, None)
    wide = P("local", None, "group")
    tall = P("local", "group", None)
    return jax.shard_map(
        body,
        mesh=mesh,
        in_specs=(tokens, tokens, tokens, tokens, wide, wide, tall),
        out_specs=(tokens, wide, wide, tall),
        check_vma=False,
    )
```

```python
import functools

import jax
import jax.numpy as jnp
from jax import lax
from jax.experimental import pallas as pl
from jax.experimental.pallas import tpu as pltpu
from jax.sharding import PartitionSpec as P

BOTH = ("group", "local")
MESH = pl.DeviceIdType.MESH
ROWS = 8
EXTRA = 128


def place(groups, local):
    me_g, me_l = lax.axis_index("group"), lax.axis_index("local")
    z, core = me_l // 2, me_l % 2
    zs = local // 2
    g_at = lambda d: lax.rem(me_g + d, groups)
    if groups == 4:
        across, along = me_g // 2, me_g % 2
        g_at = lambda d: (
            me_g, across * 2 + 1 - along, (1 - across) * 2 + along, (1 - across) * 2 + 1 - along
        )[d]
    z_at = lambda d: lax.rem(z + d, zs)
    sibling = (me_g, z * 2 + 1 - core)
    by_group = lambda d: (g_at(d), me_l)
    by_z = lambda d: (me_g, z_at(d) * 2 + core)
    return core, zs, g_at, z_at, sibling, by_group, by_z


def greet(groups, zs, sibling, by_group, by_z):
    peers = [sibling]
    peers += [by_group(d) for d in range(1, groups)]
    peers += [by_z(d) for d in range(1, zs)]
    barrier = pltpu.get_barrier_semaphore()
    for peer in peers:
        pl.semaphore_signal(barrier, inc=1, device_id=peer, device_id_type=MESH)
    pl.semaphore_wait(barrier, len(peers))


def gather_kernel(groups, local, x_in, g_in, x_out, g_out, own_sem, send_sem, recv_sem):
    core, zs, g_at, z_at, sibling, by_group, by_z = place(groups, local)
    pairs = ((x_in, x_out), (g_in, g_out))
    slot = lambda d, e, c: g_at(d) * local + z_at(e) * 2 + c
    greet(groups, zs, sibling, by_group, by_z)
    mine = slot(0, 0, core)
    sent = []

    def send(a, src, at, msg, peer):
        copy = pltpu.make_async_remote_copy(
            src_ref=src, dst_ref=pairs[a][1].at[at], send_sem=send_sem.at[a, msg],
            recv_sem=recv_sem.at[a, at], device_id=peer, device_id_type=MESH,
        )
        copy.start()
        sent.append(copy)

    def arrived(a, at):
        block = pairs[a][1].at[at]
        pltpu.make_async_remote_copy(
            src_ref=block, dst_ref=block, send_sem=send_sem.at[a, 0],
            recv_sem=recv_sem.at[a, at], device_id=sibling, device_id_type=MESH,
        ).wait_recv()

    first_group = zs - 1
    first_core = first_group + zs * (groups - 1)
    keeps = []
    relayed = groups == 4
    direct = range(1, 3 if relayed else groups)

    def relay(a, at, d, e):
        if relayed and d == 1 + e % 2:
            send(a, pairs[a][1].at[at], at, first_group + e * (groups - 1) + 2, by_group(3 - d))

    def pass_on(a, d, e):
        at = slot(d, e, core)
        arrived(a, at)
        relay(a, at, d, e)
        send(a, pairs[a][1].at[at], at, first_core + d * zs + e, sibling)

    for a in range(2):
        keep = pltpu.make_async_copy(pairs[a][0], pairs[a][1].at[mine], own_sem.at[a])
        keep.start()
        keeps.append(keep)
        for e in range(1, zs):
            send(a, pairs[a][0], mine, e - 1, by_z(e))
        for d in direct:
            send(a, pairs[a][0], mine, first_group + d - 1, by_group(d))
        send(a, pairs[a][0], mine, first_core, sibling)
    for a in range(2):
        for e in range(1, zs):
            at = slot(0, e, core)
            arrived(a, at)
            for d in direct:
                send(a, pairs[a][1].at[at], at, first_group + e * (groups - 1) + d - 1, by_group(d))
            send(a, pairs[a][1].at[at], at, first_core + e, sibling)
        for d in direct:
            pass_on(a, d, 0)
    for a in range(2):
        for e in range(1, zs):
            for d in direct:
                pass_on(a, d, e)
    for a in range(2):
        for e in range(zs):
            for d in range(3 if relayed else groups, groups):
                pass_on(a, d, e)
    for a in range(2):
        for d in range(groups):
            for e in range(zs):
                arrived(a, slot(d, e, 1 - core))
    for copy in sent:
        copy.wait_send()
    for keep in keeps:
        keep.wait()


def reduce_kernel(
    groups, local, part, out, recv_core, sum_core, recv_group, sum_z, recv_z,
    send1, got1, send2, got2, send3, got3,
):
    core, zs, g_at, z_at, sibling, by_group, by_z = place(groups, local)
    slot = lambda d, e, c: g_at(d) * local + z_at(e) * 2 + c
    greet(groups, zs, sibling, by_group, by_z)
    f32 = jnp.float32
    order = [(d, e) for e in list(range(1, zs)) + [0] for d in list(range(1, groups)) + [0]]

    def send(src, dst, s_sem, r_sem, peer):
        copy = pltpu.make_async_remote_copy(
            src_ref=src, dst_ref=dst, send_sem=s_sem, recv_sem=r_sem,
            device_id=peer, device_id_type=MESH,
        )
        copy.start()
        return copy

    first = {}
    for d, e in order:
        k = d * zs + e
        first[k] = send(
            part.at[slot(d, e, 1 - core)], recv_core.at[k], send1.at[k], got1.at[k], sibling
        )
    second = {}
    for d, e in order:
        if d == 0:
            continue
        k = d * zs + e
        first[k].wait_recv()
        both = part[slot(d, e, core)].astype(f32) + recv_core[k].astype(f32)
        sum_core[k - zs] = both.astype(sum_core.dtype)
        second[k] = send(
            sum_core.at[k - zs], recv_group.at[k - zs], send2.at[k - zs], got2.at[k - zs], by_group(d)
        )
    third = []
    for e in list(range(1, zs)) + [0]:
        first[e].wait_recv()
        total = part[slot(0, e, core)].astype(f32) + recv_core[e].astype(f32)
        for d in range(1, groups):
            k = d * zs + e
            second[k].wait_recv()
            total = total + recv_group[k - zs].astype(f32)
        if e == 0:
            out[...] = total
        else:
            sum_z[e - 1] = total.astype(sum_z.dtype)
            third.append(
                send(sum_z.at[e - 1], recv_z.at[e - 1], send3.at[e - 1], got3.at[e - 1], by_z(e))
            )
    for e in range(1, zs):
        third[e - 1].wait_recv()
        out[...] += recv_z[e - 1].astype(f32)
    for copy in [*first.values(), *second.values(), *third]:
        copy.wait_send()


def gather(groups, local, x, g):
    n = groups * local
    zs = local // 2
    messages = zs - 1 + zs * (groups - 1) + zs * groups
    anywhere = pl.BlockSpec(memory_space=pl.ANY)
    landing = pl.BlockSpec(memory_space=pltpu.VMEM)
    return pl.pallas_call(
        functools.partial(gather_kernel, groups, local),
        out_shape=(
            jax.ShapeDtypeStruct((n,) + x.shape, x.dtype),
            jax.ShapeDtypeStruct((n,) + g.shape, g.dtype),
        ),
        in_specs=[anywhere] * 2,
        out_specs=(landing, landing),
        scratch_shapes=[
            pltpu.SemaphoreType.DMA((2,)),
            pltpu.SemaphoreType.DMA((2, messages)),
            pltpu.SemaphoreType.DMA((2, n)),
        ],
        compiler_params=pltpu.CompilerParams(
            collective_id=0, has_side_effects=True, vmem_limit_bytes=50 * 2**20
        ),
        name="gather",
    )(x, g)


def reduce(groups, local, part):
    zs = local // 2
    block = part.shape[1:]
    slots = lambda k: pltpu.VMEM((k,) + block, part.dtype)
    near, far = zs * groups, zs * (groups - 1)
    dma = pltpu.SemaphoreType.DMA
    return pl.pallas_call(
        functools.partial(reduce_kernel, groups, local),
        out_shape=jax.ShapeDtypeStruct(block, jnp.float32),
        in_specs=[pl.BlockSpec(memory_space=pltpu.VMEM)],
        out_specs=pl.BlockSpec(memory_space=pltpu.VMEM),
        scratch_shapes=[
            slots(near), slots(far), slots(far), slots(zs - 1), slots(zs - 1),
            dma((near,)), dma((near,)), dma((far,)), dma((far,)), dma((zs - 1,)), dma((zs - 1,)),
        ],
        compiler_params=pltpu.CompilerParams(
            collective_id=1, has_side_effects=True, vmem_limit_bytes=50 * 2**20
        ),
        name="reduce",
    )(part)


def silu_parts(pre):
    sig = jax.nn.sigmoid(pre)
    return (pre * sig, sig * (1.0 + pre * (1.0 - sig)))


def body(features, cotangent, expert_ids, gates, w_gate, w_up, w_down):
    local = lax.axis_size("local")
    groups = lax.axis_size("group")
    tok_rows, width = features.shape
    rows = groups * local * ROWS
    pad = ROWS - tok_rows
    hits = expert_ids[..., None] == jnp.arange(local, dtype=jnp.int32)
    weight = jnp.sum(jnp.where(hits, gates[..., None], 0.0), axis=1)
    high = lax.reduce_precision(weight, 8, 7)
    middle = lax.reduce_precision(weight - high, 8, 7)
    low = weight - high - middle
    terms = jnp.concatenate([high, middle, low], axis=1).astype(jnp.bfloat16)
    terms = jnp.pad(terms, ((0, 0), (0, EXTRA - 3 * local)))
    x = jnp.pad(features, ((0, pad), (0, 0)))
    g = jnp.pad(jnp.concatenate([cotangent, terms], axis=1), ((0, pad), (0, 0)))
    all_x, all_g = gather(groups, local, x, g)
    rows_x = all_x.reshape(rows, width)
    all_g = all_g.reshape(rows, width + EXTRA)
    terms = all_g[:, width : width + 3 * local].astype(jnp.float32).reshape(rows, 3, local)
    mine = jnp.arange(local) == lax.axis_index("local")
    terms = jnp.sum(jnp.where(mine, terms, 0.0), axis=2)
    weight = (terms[:, 0] + terms[:, 1] + terms[:, 2])[:, None]
    rows_g = (weight * all_g[:, :width].astype(jnp.float32)).astype(jnp.bfloat16)
    gate_w = w_gate[0]
    up_w = w_up[0]
    down_w = w_down[0]
    pre_gate = jnp.dot(rows_x, gate_w, preferred_element_type=jnp.float32)
    pre_up = jnp.dot(rows_x, up_w, preferred_element_type=jnp.float32)
    act, slope = silu_parts(pre_gate)
    hidden = (act * pre_up).astype(jnp.bfloat16)
    d_hidden = jnp.dot(rows_g, down_w.T, preferred_element_type=jnp.float32)
    d_gate = (d_hidden * pre_up * slope).astype(jnp.bfloat16)
    d_up = (d_hidden * act).astype(jnp.bfloat16)
    part = jnp.dot(d_gate, gate_w.T, preferred_element_type=jnp.float32)
    part = part + jnp.dot(d_up, up_w.T, preferred_element_type=jnp.float32)
    part = part.astype(jnp.bfloat16).reshape(groups * local, ROWS, width)
    summed = reduce(groups, local, part)
    grad_down = jnp.dot(hidden.T, rows_g, preferred_element_type=jnp.float32).astype(jnp.bfloat16)
    grad_gate = jnp.dot(rows_x.T, d_gate, preferred_element_type=jnp.float32).astype(jnp.bfloat16)
    grad_up = jnp.dot(rows_x.T, d_up, preferred_element_type=jnp.float32).astype(jnp.bfloat16)
    return (summed[:tok_rows], grad_gate[None], grad_up[None], grad_down[None])


def solution(mesh):
    tokens = P(BOTH, None)
    wide = P("local", None, "group")
    tall = P("local", "group", None)
    return jax.shard_map(
        body,
        mesh=mesh,
        in_specs=(tokens, tokens, tokens, tokens, wide, wide, tall),
        out_specs=(tokens, wide, wide, tall),
        check_vma=False,
    )
```

```python
import functools

import jax
import jax.numpy as jnp
from jax import lax
from jax.experimental import pallas as pl
from jax.experimental.pallas import tpu as pltpu
from jax.sharding import PartitionSpec as P

BOTH = ("group", "local")
MESH = pl.DeviceIdType.MESH
ROWS = 8
EXTRA = 128


def place(groups, local):
    me_g, me_l = lax.axis_index("group"), lax.axis_index("local")
    z, core = me_l // 2, me_l % 2
    zs = local // 2
    g_at = lambda d: lax.rem(me_g + d, groups)
    if groups == 4:
        across, along = me_g // 2, me_g % 2
        g_at = lambda d: (
            me_g, across * 2 + 1 - along, (1 - across) * 2 + along, (1 - across) * 2 + 1 - along
        )[d]
    z_at = lambda d: lax.rem(z + d, zs)
    sibling = (me_g, z * 2 + 1 - core)
    by_group = lambda d: (g_at(d), me_l)
    by_z = lambda d: (me_g, z_at(d) * 2 + core)
    return core, zs, g_at, z_at, sibling, by_group, by_z


def greet(groups, zs, sibling, by_group, by_z):
    peers = [sibling]
    peers += [by_group(d) for d in range(1, groups)]
    peers += [by_z(d) for d in range(1, zs)]
    barrier = pltpu.get_barrier_semaphore()
    for peer in peers:
        pl.semaphore_signal(barrier, inc=1, device_id=peer, device_id_type=MESH)
    pl.semaphore_wait(barrier, len(peers))


def gather_kernel(groups, local, x_in, g_in, x_out, g_out, own_sem, send_sem, recv_sem):
    core, zs, g_at, z_at, sibling, by_group, by_z = place(groups, local)
    pairs = ((x_in, x_out), (g_in, g_out))
    slot = lambda d, e, c: g_at(d) * local + z_at(e) * 2 + c
    greet(groups, zs, sibling, by_group, by_z)
    mine = slot(0, 0, core)
    sent = []

    def send(a, src, at, msg, peer):
        copy = pltpu.make_async_remote_copy(
            src_ref=src, dst_ref=pairs[a][1].at[at], send_sem=send_sem.at[a, msg],
            recv_sem=recv_sem.at[a, at], device_id=peer, device_id_type=MESH,
        )
        copy.start()
        sent.append(copy)

    def arrived(a, at):
        block = pairs[a][1].at[at]
        pltpu.make_async_remote_copy(
            src_ref=block, dst_ref=block, send_sem=send_sem.at[a, 0],
            recv_sem=recv_sem.at[a, at], device_id=sibling, device_id_type=MESH,
        ).wait_recv()

    first_group = zs - 1
    first_core = first_group + zs * (groups - 1)
    keeps = []
    relayed = groups == 4
    direct = range(1, 3 if relayed else groups)

    def relay(a, at, d, e):
        if relayed and d == 1 + e % 2:
            send(a, pairs[a][1].at[at], at, first_group + e * (groups - 1) + 2, by_group(3 - d))

    def pass_on(a, d, e):
        at = slot(d, e, core)
        arrived(a, at)
        relay(a, at, d, e)
        send(a, pairs[a][1].at[at], at, first_core + d * zs + e, sibling)

    for a in range(2):
        keep = pltpu.make_async_copy(pairs[a][0], pairs[a][1].at[mine], own_sem.at[a])
        keep.start()
        keeps.append(keep)
        for e in range(1, zs):
            send(a, pairs[a][0], mine, e - 1, by_z(e))
        for d in direct:
            send(a, pairs[a][0], mine, first_group + d - 1, by_group(d))
        send(a, pairs[a][0], mine, first_core, sibling)
    for a in range(2):
        for e in range(1, zs):
            at = slot(0, e, core)
            arrived(a, at)
            for d in direct:
                send(a, pairs[a][1].at[at], at, first_group + e * (groups - 1) + d - 1, by_group(d))
            send(a, pairs[a][1].at[at], at, first_core + e, sibling)
        for d in direct:
            pass_on(a, d, 0)
    for a in range(2):
        for e in range(1, zs):
            for d in direct:
                pass_on(a, d, e)
    for a in range(2):
        for e in range(zs):
            for d in range(3 if relayed else groups, groups):
                pass_on(a, d, e)
    for a in range(2):
        for d in range(groups):
            for e in range(zs):
                arrived(a, slot(d, e, 1 - core))
    for copy in sent:
        copy.wait_send()
    for keep in keeps:
        keep.wait()


def reduce_kernel(
    groups, local, part, out, recv_core, sum_core, recv_group, sum_z, recv_z,
    send1, got1, send2, got2, send3, got3,
):
    core, zs, g_at, z_at, sibling, by_group, by_z = place(groups, local)
    slot = lambda d, e, c: g_at(d) * local + z_at(e) * 2 + c
    greet(groups, zs, sibling, by_group, by_z)
    f32 = jnp.float32
    order = [(d, e) for e in list(range(1, zs)) + [0] for d in list(range(1, groups)) + [0]]

    def send(src, dst, s_sem, r_sem, peer):
        copy = pltpu.make_async_remote_copy(
            src_ref=src, dst_ref=dst, send_sem=s_sem, recv_sem=r_sem,
            device_id=peer, device_id_type=MESH,
        )
        copy.start()
        return copy

    first = {}
    for d, e in order:
        k = d * zs + e
        first[k] = send(
            part.at[slot(d, e, 1 - core)], recv_core.at[k], send1.at[k], got1.at[k], sibling
        )
    second = {}
    for d, e in order:
        if d == 0:
            continue
        k = d * zs + e
        first[k].wait_recv()
        both = part[slot(d, e, core)].astype(f32) + recv_core[k].astype(f32)
        sum_core[k - zs] = both.astype(sum_core.dtype)
        second[k] = send(
            sum_core.at[k - zs], recv_group.at[k - zs], send2.at[k - zs], got2.at[k - zs], by_group(d)
        )
    third = []
    for e in list(range(1, zs)) + [0]:
        first[e].wait_recv()
        total = part[slot(0, e, core)].astype(f32) + recv_core[e].astype(f32)
        for d in range(1, groups):
            k = d * zs + e
            second[k].wait_recv()
            total = total + recv_group[k - zs].astype(f32)
        if e == 0:
            out[...] = total
        else:
            sum_z[e - 1] = total.astype(sum_z.dtype)
            third.append(
                send(sum_z.at[e - 1], recv_z.at[e - 1], send3.at[e - 1], got3.at[e - 1], by_z(e))
            )
    for e in range(1, zs):
        third[e - 1].wait_recv()
        out[...] += recv_z[e - 1].astype(f32)
    for copy in [*first.values(), *second.values(), *third]:
        copy.wait_send()


def gather(groups, local, x, g):
    n = groups * local
    zs = local // 2
    messages = zs - 1 + zs * (groups - 1) + zs * groups
    anywhere = pl.BlockSpec(memory_space=pl.ANY)
    return pl.pallas_call(
        functools.partial(gather_kernel, groups, local),
        out_shape=(
            jax.ShapeDtypeStruct((n,) + x.shape, x.dtype),
            jax.ShapeDtypeStruct((n,) + g.shape, g.dtype),
        ),
        in_specs=[anywhere] * 2,
        out_specs=(anywhere, anywhere),
        scratch_shapes=[
            pltpu.SemaphoreType.DMA((2,)),
            pltpu.SemaphoreType.DMA((2, messages)),
            pltpu.SemaphoreType.DMA((2, n)),
        ],
        compiler_params=pltpu.CompilerParams(collective_id=0, has_side_effects=True),
        name="gather",
    )(x, g)


def reduce(groups, local, part):
    zs = local // 2
    block = part.shape[1:]
    slots = lambda k: pltpu.VMEM((k,) + block, part.dtype)
    near, far = zs * groups, zs * (groups - 1)
    dma = pltpu.SemaphoreType.DMA
    return pl.pallas_call(
        functools.partial(reduce_kernel, groups, local),
        out_shape=jax.ShapeDtypeStruct(block, jnp.float32),
        in_specs=[pl.BlockSpec(memory_space=pltpu.VMEM)],
        out_specs=pl.BlockSpec(memory_space=pltpu.VMEM),
        scratch_shapes=[
            slots(near), slots(far), slots(far), slots(zs - 1), slots(zs - 1),
            dma((near,)), dma((near,)), dma((far,)), dma((far,)), dma((zs - 1,)), dma((zs - 1,)),
        ],
        compiler_params=pltpu.CompilerParams(
            collective_id=1, has_side_effects=True, vmem_limit_bytes=50 * 2**20
        ),
        name="reduce",
    )(part)


def silu_parts(pre):
    sig = jax.nn.sigmoid(pre)
    return (pre * sig, sig * (1.0 + pre * (1.0 - sig)))


def body(features, cotangent, expert_ids, gates, w_gate, w_up, w_down):
    local = lax.axis_size("local")
    groups = lax.axis_size("group")
    tok_rows, width = features.shape
    rows = groups * local * ROWS
    pad = ROWS - tok_rows
    hits = expert_ids[..., None] == jnp.arange(local, dtype=jnp.int32)
    weight = jnp.sum(jnp.where(hits, gates[..., None], 0.0), axis=1)
    high = lax.reduce_precision(weight, 8, 7)
    middle = lax.reduce_precision(weight - high, 8, 7)
    low = weight - high - middle
    terms = jnp.concatenate([high, middle, low], axis=1).astype(jnp.bfloat16)
    terms = jnp.pad(terms, ((0, 0), (0, EXTRA - 3 * local)))
    x = jnp.pad(features, ((0, pad), (0, 0)))
    g = jnp.pad(jnp.concatenate([cotangent, terms], axis=1), ((0, pad), (0, 0)))
    all_x, all_g = gather(groups, local, x, g)
    rows_x = all_x.reshape(rows, width)
    all_g = all_g.reshape(rows, width + EXTRA)
    terms = all_g[:, width : width + 3 * local].astype(jnp.float32).reshape(rows, 3, local)
    mine = jnp.arange(local) == lax.axis_index("local")
    terms = jnp.sum(jnp.where(mine, terms, 0.0), axis=2)
    weight = (terms[:, 0] + terms[:, 1] + terms[:, 2])[:, None]
    rows_g = (weight * all_g[:, :width].astype(jnp.float32)).astype(jnp.bfloat16)
    gate_w = w_gate[0]
    up_w = w_up[0]
    down_w = w_down[0]
    pre_gate = jnp.dot(rows_x, gate_w, preferred_element_type=jnp.float32)
    pre_up = jnp.dot(rows_x, up_w, preferred_element_type=jnp.float32)
    act, slope = silu_parts(pre_gate)
    hidden = (act * pre_up).astype(jnp.bfloat16)
    d_hidden = jnp.dot(rows_g, down_w.T, preferred_element_type=jnp.float32)
    d_gate = (d_hidden * pre_up * slope).astype(jnp.bfloat16)
    d_up = (d_hidden * act).astype(jnp.bfloat16)
    part = jnp.dot(d_gate, gate_w.T, preferred_element_type=jnp.float32)
    part = part + jnp.dot(d_up, up_w.T, preferred_element_type=jnp.float32)
    part = part.astype(jnp.bfloat16).reshape(groups * local, ROWS, width)
    summed = reduce(groups, local, part)
    grad_down = jnp.dot(hidden.T, rows_g, preferred_element_type=jnp.float32).astype(jnp.bfloat16)
    grad_gate = jnp.dot(rows_x.T, d_gate, preferred_element_type=jnp.float32).astype(jnp.bfloat16)
    grad_up = jnp.dot(rows_x.T, d_up, preferred_element_type=jnp.float32).astype(jnp.bfloat16)
    return (summed[:tok_rows], grad_gate[None], grad_up[None], grad_down[None])


def solution(mesh):
    tokens = P(BOTH, None)
    wide = P("local", None, "group")
    tall = P("local", "group", None)
    return jax.shard_map(
        body,
        mesh=mesh,
        in_specs=(tokens, tokens, tokens, tokens, wide, wide, tall),
        out_specs=(tokens, wide, wide, tall),
        check_vma=False,
    )
```
